32 devices in a mesh: shard: 8 (over z, y), dp: 4 (over x, core).
Axes of the slice: x: 2, y: 2, z: 4, core: 2. Of those that a mesh axis runs over, the one named last changes fastest.
Arguments:
- gate_up: bfloat16 [8192, 448], P(('shard', 'dp')), may hold values from -6 to 6
- route_weight: float32 [8192], P(('shard', 'dp')), may hold values from 0.1 to 1
- live_rows: int32 [32], P(('shard', 'dp')), may hold values from 1 to 256, 4915 in all
- down_weight: bfloat16 [4224, 224], P('shard'), may hold values from -0.375 to 0.375
- out_grad: bfloat16 [8192, 4224], P(('shard', 'dp')), may hold values from -6 to 6
Outputs:
- expert_out: bfloat16 [8192, 4224], P(('shard', 'dp'))
- grad_gate_up: bfloat16 [8192, 448], P(('shard', 'dp'))
- grad_route: float32 [8192], P(('shard', 'dp'))
- grad_down: float32 [4224, 224], P('shard')
The draws below stay inside these ranges and needn't reach their ends.
Inputs may be any that keep to these rules, and one draw needn't show every extreme that they name: `live_rows`: at least one device uses all 256 slots.
All inputs are finite; a program needn't handle non-finite values.
Results may differ from the reference program's by a relative error of at most 0.005.
Values may be sent and summed in bfloat16 or wider, within the bound.
A program may use at most 64 MiB of HBM per device.

```python
import math
import jax
import jax.numpy as jnp
import numpy as np
from jax import lax

D = 4224
H = 224
ROWS_DEV = 256
COUNTS = 32
ROWS = 8192


def strengthened(entries, rng, source, target, blocks, factor):
    def block_of(dim):
        return (jnp.arange(entries.shape[dim]) // (entries.shape[dim] // blocks)).reshape((-1,) + (1,) * (entries.ndim - 1 - dim))

    near = jax.random.permutation(rng, blocks)[block_of(target)]
    second = (block_of(target) + blocks // 2) % blocks
    return jnp.where((block_of(source) == near) | (block_of(source) == second), factor * entries, entries)


def block_levels(key, extent, cuts, smallest, largest):
    factor_of = 1.0
    for position, shards_of in cuts:
        draws = jax.random.uniform(jax.random.fold_in(jax.random.fold_in(key, 6), position), (shards_of,), jnp.float32, smallest / len(cuts), largest / len(cuts))
        factor_of = factor_of * jnp.repeat(jnp.exp(draws), extent[position] // shards_of).reshape((-1,) + (1,) * (len(extent) - 1 - position))
    return factor_of


def profile(amount, total, limit, lean):
    weights = [(1 << 20) // math.isqrt(grade ** lean) + 1 for grade in range(2, amount + 1)]
    spare, holding = total - limit - (amount - 1), [1] * (amount - 1)
    while spare > 0:
        candidates = [i for i in range(amount - 1) if holding[i] < limit]
        pool, left = sum([weights[i] for i in candidates]), spare
        for i in candidates:
            addition = min(limit - holding[i], max(1, left * weights[i] // pool), spare)
            holding[i] = holding[i] + addition
            spare = spare - addition
    return np.array([limit] + holding)


def uneven_parts(stream_key, count, total, bound, skew):
    if count == 2:
        one = jax.random.randint(stream_key, (), max(1, total - bound), min(bound, total - 1) + 1)
        return jnp.stack([one, total - one])
    tallies = jnp.asarray(profile(count, total, bound, skew), jnp.int32)
    couples = (count - 1) // 2
    giver, sink = tallies[1:1 + 2 * couples:2], tallies[2:2 + 2 * couples:2]
    slack = jnp.minimum(giver - 1, bound - sink)
    moved = jax.random.randint(jax.random.fold_in(stream_key, 1), (couples,), 0, 1 << 20) % (slack + 1)
    tallies = tallies.at[1:1 + 2 * couples:2].set(giver - moved).at[2:2 + 2 * couples:2].set(sink + moved)
    return tallies[jax.random.permutation(jax.random.fold_in(stream_key, 2), count)]


def bell_draw(own_key, extent, deviation, bound, shards=(), held_as=jnp.bfloat16):
    loudness = block_levels(own_key, extent, shards, -0.22, 0.18) if shards else 1.0
    entries = jax.random.normal(own_key, extent, jnp.float32) * deviation * loudness
    return jnp.minimum(jnp.maximum(entries, -bound), bound).astype(held_as)


def heavy_noise(key, dims, scale, limit, split, heavy, held_as=jnp.bfloat16):
    array = scale * jax.random.normal(key, dims, jnp.float32)
    if split:
        array = array * block_levels(key, dims, split, -0.22, 0.18)
    return jnp.clip(strengthened(array, jax.random.fold_in(key, 3), *heavy), -limit, limit).astype(held_as)


def setup_inputs(seed: int = 0) -> dict:
    seeds = jax.random.split(jax.random.key(seed), 6)
    gate_up = bell_draw(seeds[0], (ROWS, 2 * H), 1.0, 6.0, ((0, 32),))
    route_weight = jnp.clip(jnp.exp(math.log(1.0) - 2.3025851 * jax.random.uniform(seeds[1], (ROWS,), jnp.float32) ** block_levels(seeds[1], (ROWS,), ((0, 32),), -0.2, 0.2)), 0.1, 1.0)
    live_rows = uneven_parts(seeds[2], COUNTS, COUNTS * ROWS_DEV * 3 // 5, ROWS_DEV, 2).astype(jnp.int32)
    down_weight = bell_draw(seeds[3], (D, H), H ** -0.5, 0.375, ((0, 8),))
    out_grad = heavy_noise(seeds[4], (ROWS, D), 1.0, 6.0, ((0, 32),), (0, 1, 32, 2.75))
    return {"gate_up": gate_up, "route_weight": route_weight, "live_rows": live_rows, "down_weight": down_weight, "out_grad": out_grad}


def one_device(carry, inputs):
    gate_up, route_weight, live_count, out_grad, down_weight = inputs[0], inputs[1], inputs[2], inputs[3], carry[1]
    hidden_units = gate_up.shape[1] // 2
    row_mask = (jnp.arange(gate_up.shape[0], dtype=jnp.int32) < live_count).astype(jnp.float32)[:, None]
    gate_pre = gate_up[:, :hidden_units].astype(jnp.float32)
    up_proj = gate_up[:, hidden_units:].astype(jnp.float32)
    sigmoid_gate = jax.nn.sigmoid(gate_pre)
    activated = gate_pre * sigmoid_gate
    hidden = (row_mask * activated * up_proj).astype(jnp.bfloat16)
    full = lax.dot_general(hidden, down_weight, (((1,), (1,)), ((), ())), preferred_element_type=jnp.float32)
    row_scale = route_weight[:, None]
    expert_out = (row_scale * full).astype(jnp.bfloat16)
    grad_route = row_mask[:, 0] * jnp.sum(out_grad.astype(jnp.float32) * full, axis=1)
    grad_full = (row_mask * row_scale * out_grad.astype(jnp.float32)).astype(jnp.bfloat16)
    grad_hidden = jnp.dot(grad_full, down_weight, preferred_element_type=jnp.float32)
    grad_gate = grad_hidden * up_proj * sigmoid_gate * (1.0 + gate_pre * (1.0 - sigmoid_gate))
    grad_up = grad_hidden * activated
    grad_gate_up = jnp.concatenate([grad_gate, grad_up], axis=1).astype(jnp.bfloat16)
    term = lax.dot_general(grad_full, hidden, (((0,), (0,)), ((), ())), preferred_element_type=jnp.float32)
    return (carry[0] + term, down_weight), (expert_out, grad_gate_up, grad_route)


def reference(gate_up, route_weight, live_rows, down_weight, out_grad):
    devices = live_rows.shape[0]
    start = (jnp.zeros((D, H), jnp.float32), down_weight)
    stacked = (gate_up.reshape(devices, ROWS_DEV, 2 * H), route_weight.reshape(devices, ROWS_DEV),
               live_rows, out_grad.reshape(devices, ROWS_DEV, D))
    final, outputs = lax.scan(one_device, start, stacked)
    expert_out = outputs[0].reshape(devices * ROWS_DEV, D)
    grad_gate_up = outputs[1].reshape(devices * ROWS_DEV, 2 * H)
    grad_route = outputs[2].reshape(devices * ROWS_DEV)
    return expert_out, grad_gate_up, grad_route, final[0]
```

```python
import functools

import jax
import jax.numpy as jnp
from jax import lax
from jax.experimental import pallas as pl
from jax.experimental.pallas import tpu as pltpu
from jax.sharding import PartitionSpec as P

LANES = 128
F32 = jnp.float32
BF16 = jnp.bfloat16


def kernel(
    gate_up, route_weight, live_rows, weight, out_grad,
    expert_out, grad_gate_up, grad_route, grad_down,
    og, gf, eo, hid, wg, acc, psend, crecv,
    xs0, xr0, ys0, yr0, xs1, xr1, ys1, yr1, zs, zr, fin,
    og_sem, eo_sem, w_recv, w_send, r_recv, r_send, z_recv, f_recv,
):
    slots, features = og.shape
    own_rows = weight.shape[0]
    units = weight.shape[1]
    region = 2 * own_rows
    chunk = 3 * LANES
    chunks = features // chunk
    first_half = (2 * region + chunk - 1) // chunk

    me_s, me_d = lax.axis_index("shard"), lax.axis_index("dp")
    z, y, x, c = me_s // 2, me_s % 2, me_d // 2, me_d % 2
    home = lax.rem(z, 2) == c

    def device(zz, yy, xx, cc):
        return (zz * 2 + yy, xx * 2 + cc)

    to_x, to_y, to_c = device(z, y, 1 - x, c), device(z, 1 - y, x, c), device(z, y, x, 1 - c)
    others_z = [lax.rem(z + d, 4) for d in (1, 2, 3)]

    def rows(zz, yy):
        return pl.ds(pl.multiple_of((zz * 2 + yy) * own_rows, 16), own_rows)

    def plane(zz):
        return pl.ds(pl.multiple_of(zz * region, 16), region)

    def remote(src, dst, send, recv, dev):
        return pltpu.make_async_remote_copy(
            src_ref=src, dst_ref=dst, send_sem=send, recv_sem=recv,
            device_id=dev, device_id_type=pl.DeviceIdType.MESH,
        )

    load = pltpu.make_async_copy(out_grad, og, og_sem)
    load.start()
    barrier = pltpu.get_barrier_semaphore()
    partners = [to_x, to_y, to_c] + [device(zz, y, x, c) for zz in others_z]

    wg[0, rows(z, y), :] = weight[:, :LANES]
    wg[1, rows(z, y), :] = jnp.concatenate(
        [weight[:, LANES:], jnp.zeros((own_rows, 2 * LANES - units), BF16)], axis=1
    )
    for dev in partners:
        pl.semaphore_signal(barrier, inc=1, device_id=dev, device_id_type=pl.DeviceIdType.MESH)

    live = (lax.broadcasted_iota(jnp.int32, (slots, LANES), 0) < live_rows[0]).astype(F32)
    scale = jnp.broadcast_to(route_weight[...], (LANES, slots)).T
    live_scale = live * scale

    def gates():
        both = gate_up[...].astype(F32)
        gate, up = both[:, :units], both[:, units:]
        sig = jax.nn.sigmoid(gate)
        return gate, up, sig, gate * sig

    _, up, _, activated = gates()
    hidden = live[:, :1] * activated * up
    hid[...] = jnp.concatenate(
        [hidden, jnp.zeros((slots, 2 * LANES - units), F32)], axis=1
    ).astype(BF16)
    pl.semaphore_wait(barrier, len(partners))

    pending = []
    count = {"w": 0, "r": 0}

    def begin(kind, src, dst, recv, dev, cond=None):
        sems = w_send if kind == "w" else r_send
        copy = remote(src, dst, sems.at[count[kind]], recv, dev)
        count[kind] += 1
        pending.append((copy, cond))
        if cond is None:
            copy.start()
        else:
            pl.when(cond)(copy.start)

    def arrived(ref, recv, cond=None):
        copy = remote(ref, ref, w_send.at[0], recv, to_x)
        if cond is None:
            copy.wait_recv()
        else:
            pl.when(cond)(copy.wait_recv)

    def w_piece(zz, yy, t):
        return wg.at[t, rows(zz, yy)], w_recv.at[t, zz * 2 + yy]

    def w_give(zz, yy, t, dev, cond=None):
        ref, sem = w_piece(zz, yy, t)
        begin("w", ref, ref, sem, dev, cond)

    def w_take(zz, yy, t, cond=None):
        ref, sem = w_piece(zz, yy, t)
        arrived(ref, sem, cond)

    for zz in others_z:
        w_give(z, y, x, device(zz, y, x, c), home)

    load.wait()
    wide = jnp.concatenate([live_scale] * 3, axis=1)

    def partial(i, carry):
        at = pl.ds(pl.multiple_of(i * chunk, LANES), chunk)
        g = (wide * og[:, at].astype(F32)).astype(BF16)
        gf[:, at] = g
        p = lax.dot_general(g, hid[...], (((0,), (0,)), ((), ())), preferred_element_type=F32)
        for t in (0, 1):
            part = p[:, t * LANES:(t + 1) * LANES]
            acc[t, at, :] = part
            psend[t, at, :] = part.astype(BF16)
        return carry

    for k, (low, high) in enumerate(((0, first_half), (first_half, chunks))):
        lax.fori_loop(low, high, partial, 0)
        for t in (0, 1):
            begin("r", psend.at[t, plane(1 - c + 2 * k)], crecv.at[t, k], r_recv.at[2 * k + t], to_c)

    zk = [c, c + 2]
    far = [zk[0] != z, zk[1] != z]

    for t in (0, 1):
        arrived(crecv.at[t, 0], r_recv.at[t])
    xs0[...] = (acc[1 - x, plane(zk[0]), :] + crecv[1 - x, 0].astype(F32)).astype(BF16)
    begin("r", xs0, xr0, r_recv.at[4], to_x)
    acc[x, plane(zk[0]), :] += crecv[x, 0].astype(F32)
    for t in (0, 1):
        arrived(crecv.at[t, 1], r_recv.at[2 + t])

    def half(yy):
        return pl.ds(pl.multiple_of(yy * own_rows, 16), own_rows)

    for t in (0, 1):
        ys1[t] = (acc[t, rows(zk[1], 1 - y), :] + crecv[t, 1, half(1 - y), :].astype(F32)).astype(BF16)
    begin("r", ys1, yr1, r_recv.at[5], to_y)
    for t in (0, 1):
        acc[t, rows(zk[1], y), :] += crecv[t, 1, half(y), :].astype(F32)

    w_take(zk[0], y, x, far[0])
    w_give(zk[0], y, x, to_y)
    w_give(zk[0], y, x, to_x, far[0])
    w_give(zk[0], y, x, to_c, far[0])
    w_take(zk[1], y, x, far[1])
    w_give(zk[1], y, x, to_x, far[1])
    w_give(zk[1], y, x, to_y)
    w_give(zk[1], y, x, to_c, far[1])

    arrived(xr0, r_recv.at[4])
    ys0[...] = (acc[x, rows(zk[0], 1 - y), :] + xr0[half(1 - y), :].astype(F32)).astype(BF16)
    begin("r", ys0, yr0, r_recv.at[6], to_y)
    acc[x, rows(zk[0], y), :] += xr0[half(y), :].astype(F32)
    arrived(yr1, r_recv.at[5])
    xs1[...] = (acc[1 - x, rows(zk[1], y), :] + yr1[1 - x].astype(F32)).astype(BF16)
    begin("r", xs1, xr1, r_recv.at[7], to_x)
    acc[x, rows(zk[1], y), :] += yr1[x].astype(F32)

    w_take(zk[0], 1 - y, x)
    w_give(zk[0], 1 - y, x, to_x)
    w_give(zk[0], 1 - y, x, to_c)
    w_take(zk[1], y, 1 - x, far[1])
    w_give(zk[1], y, 1 - x, to_y)
    w_give(zk[1], y, 1 - x, to_c, far[1])
    w_take(zk[0], y, 1 - x, far[0])
    w_give(zk[0], y, 1 - x, to_c, far[0])
    w_take(zk[1], 1 - y, x)
    w_give(zk[1], 1 - y, x, to_c)

    for k, buf in ((0, yr0), (1, xr1)):
        arrived(buf, r_recv.at[6 + k])
        acc[x, rows(zk[k], y), :] += buf[...].astype(F32)
        zs[k] = acc[x, rows(zk[k], y), :].astype(BF16)
        begin("r", zs.at[k], zr.at[z], z_recv.at[z], device(zk[k], y, x, c), far[k])

    w_take(zk[0], 1 - y, 1 - x)
    w_give(zk[0], 1 - y, 1 - x, to_c)
    w_take(zk[1], 1 - y, 1 - x)
    w_give(zk[1], 1 - y, 1 - x, to_c)

    away = jnp.logical_not(home)

    @pl.when(home)
    def _():
        total = acc[x, rows(z, y), :]
        for zz in others_z:
            arrived(zr.at[zz], z_recv.at[zz])
            total = total + zr[zz].astype(F32)
        fin[x] = total

    begin("r", fin.at[x], fin.at[x], f_recv.at[x], to_x, home)
    begin("r", fin.at[x], fin.at[x], f_recv.at[x], to_c, home)

    for k in (0, 1):
        zz = 1 - c + 2 * k
        for yy in (0, 1):
            mine = jnp.logical_and(zz == z, yy == y)
            for t in (0, 1):
                w_take(zz, yy, t, jnp.logical_not(mine))

    wide_route = jnp.concatenate([scale] * 3, axis=1)

    def store(i):
        at = pl.ds(pl.multiple_of(i * chunk, LANES), chunk)
        return pltpu.make_async_copy(eo.at[:, at], expert_out.at[:, at], eo_sem.at[i])

    def outputs(i, carry):
        grad_hidden, route = carry
        at = pl.ds(pl.multiple_of(i * chunk, LANES), chunk)
        w = jnp.concatenate([wg[0, at, :], wg[1, at, :]], axis=1)
        full = lax.dot_general(hid[...], w, (((1,), (1,)), ((), ())), preferred_element_type=F32)
        eo[:, at] = (wide_route * full).astype(BF16)
        prod = og[:, at].astype(F32) * full
        route = route + prod[:, :LANES] + prod[:, LANES:2 * LANES] + prod[:, 2 * LANES:]
        grad_hidden = grad_hidden + jnp.dot(gf[:, at], w, preferred_element_type=F32)
        store(i).start()
        return grad_hidden, route

    grad_hidden, route = lax.fori_loop(
        0, chunks, outputs,
        (jnp.zeros((slots, 2 * LANES), F32), jnp.zeros((slots, LANES), F32)),
    )
    grad_route[...] = jnp.sum((live * route).T, axis=0, keepdims=True)
    gate, up, sig, activated = gates()
    grad_hidden = grad_hidden[:, :units]
    grad_gate = grad_hidden * up * sig * (1.0 + gate * (1.0 - sig))
    grad_gate_up[...] = jnp.concatenate([grad_gate, grad_hidden * activated], axis=1).astype(BF16)

    arrived(fin.at[1 - x], f_recv.at[1 - x], home)
    begin("r", fin.at[1 - x], fin.at[1 - x], f_recv.at[1 - x], to_c, home)
    arrived(fin.at[x], f_recv.at[x], away)
    arrived(fin.at[1 - x], f_recv.at[1 - x], away)
    grad_down[:, :LANES] = fin[0]
    grad_down[:, LANES:] = fin[1, :, :units - LANES]

    for copy, cond in pending:
        if cond is None:
            copy.wait_send()
        else:
            pl.when(cond)(copy.wait_send)

    def drain(i, carry):
        store(i).wait()
        return carry

    lax.fori_loop(0, chunks, drain, 0)


def fused(gate_up, route_weight, live_rows, down_weight, out_grad):
    slots, features = out_grad.shape
    own_rows, units = down_weight.shape
    region = 2 * own_rows
    chunks = features // (3 * LANES)
    vmem = functools.partial(pl.BlockSpec, memory_space=pltpu.VMEM)
    hbm = functools.partial(pl.BlockSpec, memory_space=pl.ANY)
    dma = pltpu.SemaphoreType.DMA
    expert_out, grad_gate_up, grad_route, grad_down = pl.pallas_call(
        kernel,
        out_shape=(
            jax.ShapeDtypeStruct((slots, features), BF16),
            jax.ShapeDtypeStruct(gate_up.shape, BF16),
            jax.ShapeDtypeStruct((1, slots), F32),
            jax.ShapeDtypeStruct((own_rows, units), F32),
        ),
        in_specs=[vmem(), vmem(), pl.BlockSpec(memory_space=pltpu.SMEM), vmem(), hbm()],
        out_specs=(hbm(), vmem(), vmem(), vmem()),
        scratch_shapes=[
            pltpu.VMEM((slots, features), BF16),
            pltpu.VMEM((slots, features), BF16),
            pltpu.VMEM((slots, features), BF16),
            pltpu.VMEM((slots, 2 * LANES), BF16),
            pltpu.VMEM((2, features, LANES), BF16),
            pltpu.VMEM((2, features, LANES), F32),
            pltpu.VMEM((2, features, LANES), BF16),
            pltpu.VMEM((2, 2, region, LANES), BF16),
            pltpu.VMEM((region, LANES), BF16),
            pltpu.VMEM((region, LANES), BF16),
            pltpu.VMEM((own_rows, LANES), BF16),
            pltpu.VMEM((own_rows, LANES), BF16),
            pltpu.VMEM((own_rows, LANES), BF16),
            pltpu.VMEM((own_rows, LANES), BF16),
            pltpu.VMEM((2, own_rows, LANES), BF16),
            pltpu.VMEM((2, own_rows, LANES), BF16),
            pltpu.VMEM((2, own_rows, LANES), BF16),
            pltpu.VMEM((4, own_rows, LANES), BF16),
            pltpu.VMEM((2, own_rows, LANES), F32),
            dma, dma((chunks,)), dma((2, 8)), dma((24,)), dma((8,)), dma((16,)), dma((4,)), dma((2,)),
        ],
        compiler_params=pltpu.CompilerParams(
            collective_id=0, has_side_effects=True, vmem_limit_bytes=40 * 2**20
        ),
        cost_estimate=pl.CostEstimate(
            flops=6 * slots * features * units, bytes_accessed=6 * slots * features, transcendentals=0
        ),
    )(gate_up, route_weight.reshape(1, slots), live_rows, down_weight, out_grad)
    return expert_out, grad_gate_up, grad_route.reshape(slots), grad_down


def plain(gate_up, route_weight, live_rows, down_weight, out_grad):
    slot_count = gate_up.shape[0]
    hidden_units = gate_up.shape[1] // 2
    row_mask = (lax.iota(jnp.int32, slot_count) < live_rows[0]).astype(jnp.float32)[:, None]
    gate_pre = gate_up[:, :hidden_units].astype(jnp.float32)
    up_proj = gate_up[:, hidden_units:].astype(jnp.float32)
    sigmoid_gate = jax.nn.sigmoid(gate_pre)
    activated = gate_pre * sigmoid_gate
    hidden = (row_mask * activated * up_proj).astype(jnp.bfloat16)
    row_scale = route_weight[:, None]
    gathered = lax.all_gather(down_weight, "shard", axis=0, tiled=True)
    full = lax.dot_general(
        hidden, gathered, (((1,), (1,)), ((), ())), preferred_element_type=jnp.float32
    )
    expert_out = (row_scale * full).astype(jnp.bfloat16)
    grad_route = row_mask[:, 0] * jnp.sum(out_grad.astype(jnp.float32) * full, axis=1)
    grad_full = (row_mask * row_scale * out_grad.astype(jnp.float32)).astype(jnp.bfloat16)
    grad_hidden = jnp.dot(grad_full, gathered, preferred_element_type=jnp.float32)
    grad_gate = grad_hidden * up_proj * sigmoid_gate * (1.0 + gate_pre * (1.0 - sigmoid_gate))
    grad_up = grad_hidden * activated
    grad_gate_up = jnp.concatenate([grad_gate, grad_up], axis=1).astype(jnp.bfloat16)
    owned = lax.psum_scatter(
        lax.dot_general(
            grad_full, hidden, (((0,), (0,)), ((), ())), preferred_element_type=jnp.float32
        ),
        "shard",
        scatter_dimension=0,
        tiled=True,
    )
    grad_down = lax.psum(owned, "dp")
    return (expert_out, grad_gate_up, grad_route, grad_down)


def solution(mesh):
    shape = (mesh.shape["shard"], mesh.shape["dp"])
    in_specs = (
        P(("shard", "dp"), None),
        P(("shard", "dp")),
        P(("shard", "dp")),
        P("shard", None),
        P(("shard", "dp"), None),
    )
    out_specs = (
        P(("shard", "dp"), None),
        P(("shard", "dp"), None),
        P(("shard", "dp")),
        P("shard", None),
    )
    return jax.shard_map(
        fused if shape == (8, 4) else plain,
        mesh=mesh, in_specs=in_specs, out_specs=out_specs, check_vma=False,
    )
```

```python
import jax
import jax.numpy as jnp
from jax import lax
from jax.experimental import pallas as pl
from jax.experimental.pallas import tpu as pltpu
from jax.sharding import PartitionSpec as P

LANES = 128
F32 = jnp.float32
BF16 = jnp.bfloat16


def kernel(
    gate_up, route_weight, live_rows, weight, out_grad,
    eo, grad_gate_up, grad_route, grad_down,
    og, gu, rw, wt, gf, hid, wg, acc, psend, crecv,
    xs0, xr0, ys0, yr0, xs1, xr1, ys1, yr1, zs, zr, tot, fin,
    in_sem, w_recv, w_send, c_recv, r_recv, h_recv, r_send, z_recv, f_recv,
):
    slots, features = og.shape
    own_rows = wt.shape[0]
    units = wt.shape[1]
    region = 2 * own_rows
    chunk = 3 * LANES
    chunks = features // chunk
    first_half = (2 * region + chunk - 1) // chunk
    split = (own_rows // 2 + 15) // 16 * 16
    halves = [pl.ds(0, split), pl.ds(split, own_rows - split)]

    loads = [
        pltpu.make_async_copy(src, dst, in_sem.at[i])
        for i, (src, dst) in enumerate(
            ((weight, wt), (gate_up, gu), (route_weight, rw), (out_grad, og))
        )
    ]
    for copy in loads:
        copy.start()

    me_s, me_d = lax.axis_index("shard"), lax.axis_index("dp")
    z, y, x, c = me_s // 2, me_s % 2, me_d // 2, me_d % 2
    home = lax.rem(z, 2) == c
    away = jnp.logical_not(home)

    def device(zz, yy, xx, cc):
        return (zz * 2 + yy, xx * 2 + cc)

    to_x, to_y, to_c = device(z, y, 1 - x, c), device(z, 1 - y, x, c), device(z, y, x, 1 - c)
    others_z = [lax.rem(z + d, 4) for d in (1, 2, 3)]

    barrier = pltpu.get_barrier_semaphore()
    partners = [to_x, to_y, to_c] + [device(zz, y, x, c) for zz in others_z]
    for dev in partners:
        pl.semaphore_signal(barrier, inc=1, device_id=dev, device_id_type=pl.DeviceIdType.MESH)

    def rows(zz, yy):
        return pl.ds(pl.multiple_of((zz * 2 + yy) * own_rows, 16), own_rows)

    def rows_of(zz, yy, part):
        return pl.ds(pl.multiple_of((zz * 2 + yy) * own_rows + part.start, 16), part.size)

    def plane(zz):
        return pl.ds(pl.multiple_of(zz * region, 16), region)

    pending = []
    count = {"w": 0, "r": 0}

    def begin(kind, src, dst, recv, dev, cond=None):
        sems = w_send if kind == "w" else r_send
        copy = pltpu.make_async_remote_copy(
            src_ref=src, dst_ref=dst, send_sem=sems.at[count[kind]], recv_sem=recv,
            device_id=dev, device_id_type=pl.DeviceIdType.MESH,
        )
        count[kind] += 1
        pending.append((copy, cond))
        if cond is None:
            copy.start()
        else:
            pl.when(cond)(copy.start)

    def arrived(ref, recv, cond=None):
        copy = pltpu.make_async_remote_copy(
            src_ref=ref, dst_ref=ref, send_sem=w_send.at[0], recv_sem=recv,
            device_id=to_x, device_id_type=pl.DeviceIdType.MESH,
        )
        if cond is None:
            copy.wait_recv()
        else:
            pl.when(cond)(copy.wait_recv)

    def w_piece(zz, yy, t):
        return wg.at[t, rows(zz, yy)], w_recv.at[t, zz * 2 + yy]

    def w_give(zz, yy, t, dev, cond=None):
        ref, sem = w_piece(zz, yy, t)
        begin("w", ref, ref, sem, dev, cond)

    def w_take(zz, yy, t, cond=None):
        ref, sem = w_piece(zz, yy, t)
        arrived(ref, sem, cond)

    loads[0].wait()
    wg[0, rows(z, y), :] = wt[:, :LANES]
    wg[1, rows(z, y), :] = jnp.concatenate(
        [wt[:, LANES:], jnp.zeros((own_rows, 2 * LANES - units), BF16)], axis=1
    )
    pl.semaphore_wait(barrier, len(partners))

    zk = [c, c + 2]
    far = [zk[0] != z, zk[1] != z]
    near = [zk[0] == z, zk[1] == z]

    for zz in others_z:
        w_give(z, y, x, device(zz, y, x, c), home)
    w_give(z, y, x, to_y, home)

    loads[1].wait()
    loads[2].wait()

    def gates():
        gate, up = gu[:units, :].astype(F32), gu[units:, :].astype(F32)
        sig = jax.nn.sigmoid(gate)
        return gate, up, sig, gate * sig

    _, up, _, activated = gates()
    live_row = (lax.broadcasted_iota(jnp.int32, (1, slots), 1) < live_rows[0]).astype(F32)
    hidden = live_row * activated * up
    hid[...] = jnp.concatenate(
        [hidden, jnp.zeros((2 * LANES - units, slots), F32)], axis=0
    ).T.astype(BF16)
    live = (lax.broadcasted_iota(jnp.int32, (slots, LANES), 0) < live_rows[0]).astype(F32)
    scale = jnp.broadcast_to(rw[...], (LANES, slots)).T
    wide = jnp.concatenate([live * scale] * 3, axis=1)
    loads[3].wait()

    def partial(i, carry):
        at = pl.ds(pl.multiple_of(i * chunk, LANES), chunk)
        g = (wide * og[:, at].astype(F32)).astype(BF16)
        gf[:, at] = g
        p = lax.dot_general(g, hid[...], (((0,), (0,)), ((), ())), preferred_element_type=F32)
        for t in (0, 1):
            part = p[:, t * LANES:(t + 1) * LANES]
            acc[t, at, :] = part
            psend[t, at, :] = part.astype(BF16)
        return carry

    for k, (low, high) in enumerate(((0, first_half), (first_half, chunks))):
        lax.fori_loop(low, high, partial, 0)
        for t in (0, 1):
            begin("r", psend.at[t, plane(1 - c + 2 * k)], crecv.at[t, k], c_recv.at[k, t], to_c)

    def pair(t, k, yy, part=None):
        part = pl.ds(0, own_rows) if part is None else part
        there = pl.ds(pl.multiple_of(yy * own_rows + part.start, 16), part.size)
        return acc[t, rows_of(zk[k], yy, part), :] + crecv[t, k, there, :].astype(F32)

    for t in (0, 1):
        arrived(crecv.at[t, 0], c_recv.at[0, t])
    for i, yy in enumerate((1 - y, y)):
        xs0[i] = pair(1 - x, 0, yy).astype(BF16)
        begin("r", xs0.at[i], xr0.at[i], r_recv.at[0, i], to_x)
    for t in (0, 1):
        arrived(crecv.at[t, 1], c_recv.at[1, t])
    for i, t in enumerate((1 - x, x)):
        ys1[i] = pair(t, 1, 1 - y).astype(BF16)
        begin("r", ys1.at[i], yr1.at[i], r_recv.at[1, i], to_y)

    w_take(zk[0], y, x, far[0])
    w_give(zk[0], y, x, to_y, far[0])
    w_give(zk[0], y, x, to_x, far[0])
    w_give(zk[0], y, x, to_c, far[0])
    w_take(zk[1], y, x, far[1])
    w_give(zk[1], y, x, to_x, far[1])
    w_give(zk[1], y, x, to_y, far[1])
    w_give(zk[1], y, x, to_c, far[1])

    arrived(xr0.at[0], r_recv.at[0, 0])
    for h, part in enumerate(halves):
        ys0[part, :] = (pair(x, 0, 1 - y, part) + xr0[0, part, :].astype(F32)).astype(BF16)
        begin("r", ys0.at[part], yr0.at[part], h_recv.at[0, h], to_y)
    arrived(yr1.at[0], r_recv.at[1, 0])
    for h, part in enumerate(halves):
        xs1[part, :] = (pair(1 - x, 1, y, part) + yr1[0, part, :].astype(F32)).astype(BF16)
        begin("r", xs1.at[part], xr1.at[part], h_recv.at[1, h], to_x)

    w_take(zk[0], 1 - y, x)
    w_give(zk[0], 1 - y, x, to_x)
    w_give(zk[0], 1 - y, x, to_c)
    w_take(zk[1], y, 1 - x, far[1])
    w_give(zk[1], y, 1 - x, to_y)
    w_give(zk[1], y, 1 - x, to_c, far[1])
    w_take(zk[0], y, 1 - x, far[0])
    w_give(zk[0], y, 1 - x, to_c, far[0])
    w_take(zk[1], 1 - y, x)
    w_give(zk[1], 1 - y, x, to_c)

    arrived(xr0.at[1], r_recv.at[0, 1])
    arrived(yr1.at[1], r_recv.at[1, 1])
    for h, part in enumerate(halves):
        for k, (first, second) in enumerate(((xr0, yr0), (yr1, xr1))):
            arrived(second.at[part], h_recv.at[k, h])
            total = (
                pair(x, k, y, part) + first[1, part, :].astype(F32) + second[part, :].astype(F32)
            )
            zs[k, part, :] = total.astype(BF16)
            begin("r", zs.at[k, part], zr.at[z, part], z_recv.at[h, z], device(zk[k], y, x, c), far[k])

            @pl.when(near[k])
            def _():
                tot[part, :] = total

    w_take(zk[0], 1 - y, 1 - x)
    w_give(zk[0], 1 - y, 1 - x, to_c)
    w_take(zk[1], 1 - y, 1 - x)
    w_give(zk[1], 1 - y, 1 - x, to_c)
    for k in (0, 1):
        zz = 1 - c + 2 * k
        for yy in (0, 1):
            mine = jnp.logical_and(zz == z, yy == y)
            for t in (0, 1):
                w_take(zz, yy, t, jnp.logical_not(mine))

    wide_route = jnp.concatenate([scale] * 3, axis=1)

    def outputs(i, carry):
        grad_hidden, route = carry
        at = pl.ds(pl.multiple_of(i * chunk, LANES), chunk)
        w = jnp.concatenate([wg[0, at, :], wg[1, at, :]], axis=1)
        full = lax.dot_general(hid[...], w, (((1,), (1,)), ((), ())), preferred_element_type=F32)
        eo[:, at] = (wide_route * full).astype(BF16)
        prod = og[:, at].astype(F32) * full
        route = route + prod[:, :LANES] + prod[:, LANES:2 * LANES] + prod[:, 2 * LANES:]
        grad_hidden = grad_hidden + jnp.dot(gf[:, at], w, preferred_element_type=F32)
        return grad_hidden, route

    grad_hidden, route = lax.fori_loop(
        0, chunks, outputs,
        (jnp.zeros((slots, 2 * LANES), F32), jnp.zeros((slots, LANES), F32)),
    )
    grad_route[...] = jnp.sum((live * route).T, axis=0, keepdims=True)
    gate, up, sig, activated = gates()
    grad_hidden = grad_hidden.T[:units, :]
    grad_gate_up[:units, :] = (grad_hidden * up * sig * (1.0 + gate * (1.0 - sig))).astype(BF16)
    grad_gate_up[units:, :] = (grad_hidden * activated).astype(BF16)

    for h, part in enumerate(halves):
        @pl.when(home)
        def _():
            total = tot[part, :]
            for zz in others_z:
                arrived(zr.at[zz, part], z_recv.at[h, zz])
                total = total + zr[zz, part, :].astype(F32)
            fin[x, part, :] = total

        begin("r", fin.at[x, part], fin.at[x, part], f_recv.at[h, x], to_x, home)
        begin("r", fin.at[x, part], fin.at[x, part], f_recv.at[h, x], to_c, home)
    for h, part in enumerate(halves):
        arrived(fin.at[1 - x, part], f_recv.at[h, 1 - x], home)
        begin("r", fin.at[1 - x, part], fin.at[1 - x, part], f_recv.at[h, 1 - x], to_c, home)
    for h, part in enumerate(halves):
        arrived(fin.at[x, part], f_recv.at[h, x], away)
        arrived(fin.at[1 - x, part], f_recv.at[h, 1 - x], away)
    grad_down[:, :LANES] = fin[0]
    grad_down[:, LANES:] = fin[1, :, :units - LANES]

    for copy, cond in pending:
        if cond is None:
            copy.wait_send()
        else:
            pl.when(cond)(copy.wait_send)


def place(*refs):
    count = (len(refs) - 1) // 2
    copies = [
        pltpu.make_async_copy(refs[i], refs[count + i], refs[-1].at[i]) for i in range(count)
    ]
    for copy in copies:
        copy.start()
    for copy in copies:
        copy.wait()


def fused(gate_up, route_weight, live_rows, down_weight, out_grad):
    slots, features = out_grad.shape
    own_rows, units = down_weight.shape
    region = 2 * own_rows
    vmem = pl.BlockSpec(memory_space=pltpu.VMEM)
    hbm = pl.BlockSpec(memory_space=pltpu.HBM)
    dma = pltpu.SemaphoreType.DMA
    piece = (own_rows, LANES)
    shapes = (
        jax.ShapeDtypeStruct((slots, features), BF16),
        jax.ShapeDtypeStruct((2 * units, slots), BF16),
        jax.ShapeDtypeStruct((1, slots), F32),
        jax.ShapeDtypeStruct((own_rows, units), F32),
    )
    results = pl.pallas_call(
        kernel,
        out_shape=tuple(pltpu.VMEM(a.shape, a.dtype) for a in shapes),
        in_specs=[hbm, hbm, pl.BlockSpec(memory_space=pltpu.SMEM), hbm, hbm],
        out_specs=(vmem,) * 4,
        scratch_shapes=[
            pltpu.VMEM((slots, features), BF16),
            pltpu.VMEM((2 * units, slots), BF16),
            pltpu.VMEM((1, slots), F32),
            pltpu.VMEM((own_rows, units), BF16),
            pltpu.VMEM((slots, features), BF16),
            pltpu.VMEM((slots, 2 * LANES), BF16),
            pltpu.VMEM((2, features, LANES), BF16),
            pltpu.VMEM((2, features, LANES), F32),
            pltpu.VMEM((2, features, LANES), BF16),
            pltpu.VMEM((2, 2, region, LANES), BF16),
            pltpu.VMEM((2,) + piece, BF16),
            pltpu.VMEM((2,) + piece, BF16),
            pltpu.VMEM(piece, BF16),
            pltpu.VMEM(piece, BF16),
            pltpu.VMEM(piece, BF16),
            pltpu.VMEM(piece, BF16),
            pltpu.VMEM((2,) + piece, BF16),
            pltpu.VMEM((2,) + piece, BF16),
            pltpu.VMEM((2,) + piece, BF16),
            pltpu.VMEM((4,) + piece, BF16),
            pltpu.VMEM(piece, F32),
            pltpu.VMEM((2,) + piece, F32),
            dma((4,)), dma((2, 8)), dma((24,)), dma((2, 2)), dma((2, 2)), dma((2, 2)),
            dma((24,)), dma((2, 4)), dma((2, 2)),
        ],
        compiler_params=pltpu.CompilerParams(
            collective_id=0, has_side_effects=True, vmem_limit_bytes=58 * 2**20
        ),
        cost_estimate=pl.CostEstimate(
            flops=6 * slots * features * units, bytes_accessed=6 * slots * features, transcendentals=0
        ),
    )(gate_up.T, route_weight.reshape(1, slots), live_rows, down_weight, out_grad)
    expert_out, grad_gate_up, grad_route, grad_down = pl.pallas_call(
        place,
        out_shape=shapes,
        in_specs=[pl.BlockSpec(memory_space=pl.ANY)] * 4,
        out_specs=(hbm,) * 4,
        scratch_shapes=[dma((4,))],
        compiler_params=pltpu.CompilerParams(vmem_limit_bytes=2**20),
    )(*results)
    return expert_out, grad_gate_up.T, grad_route.reshape(slots), grad_down


def plain(gate_up, route_weight, live_rows, down_weight, out_grad):
    slot_count = gate_up.shape[0]
    hidden_units = gate_up.shape[1] // 2
    row_mask = (lax.iota(jnp.int32, slot_count) < live_rows[0]).astype(jnp.float32)[:, None]
    gate_pre = gate_up[:, :hidden_units].astype(jnp.float32)
    up_proj = gate_up[:, hidden_units:].astype(jnp.float32)
    sigmoid_gate = jax.nn.sigmoid(gate_pre)
    activated = gate_pre * sigmoid_gate
    hidden = (row_mask * activated * up_proj).astype(jnp.bfloat16)
    row_scale = route_weight[:, None]
    gathered = lax.all_gather(down_weight, "shard", axis=0, tiled=True)
    full = lax.dot_general(
        hidden, gathered, (((1,), (1,)), ((), ())), preferred_element_type=jnp.float32
    )
    expert_out = (row_scale * full).astype(jnp.bfloat16)
    grad_route = row_mask[:, 0] * jnp.sum(out_grad.astype(jnp.float32) * full, axis=1)
    grad_full = (row_mask * row_scale * out_grad.astype(jnp.float32)).astype(jnp.bfloat16)
    grad_hidden = jnp.dot(grad_full, gathered, preferred_element_type=jnp.float32)
    grad_gate = grad_hidden * up_proj * sigmoid_gate * (1.0 + gate_pre * (1.0 - sigmoid_gate))
    grad_up = grad_hidden * activated
    grad_gate_up = jnp.concatenate([grad_gate, grad_up], axis=1).astype(jnp.bfloat16)
    owned = lax.psum_scatter(
        lax.dot_general(
            grad_full, hidden, (((0,), (0,)), ((), ())), preferred_element_type=jnp.float32
        ),
        "shard",
        scatter_dimension=0,
        tiled=True,
    )
    grad_down = lax.psum(owned, "dp")
    return (expert_out, grad_gate_up, grad_route, grad_down)


def solution(mesh):
    shape = (mesh.shape["shard"], mesh.shape["dp"])
    in_specs = (
        P(("shard", "dp"), None),
        P(("shard", "dp")),
        P(("shard", "dp")),
        P("shard", None),
        P(("shard", "dp"), None),
    )
    out_specs = (
        P(("shard", "dp"), None),
        P(("shard", "dp"), None),
        P(("shard", "dp")),
        P("shard", None),
    )
    return jax.shard_map(
        fused if shape == (8, 4) else plain,
        mesh=mesh, in_specs=in_specs, out_specs=out_specs, check_vma=False,
    )
```

```python
import jax
import jax.numpy as jnp
from jax import lax
from jax.experimental import pallas as pl
from jax.experimental.pallas import tpu as pltpu
from jax.sharding import PartitionSpec as P

LANES = 128
SLICES = 3
F32 = jnp.float32
BF16 = jnp.bfloat16


def kernel(
    gate_up, route_weight, live_rows, weight, out_grad,
    eo, grad_gate_up, grad_route, grad_down,
    og, gu, rw, wt, gf, hid, wg, acc, psend, crecv,
    xs0, xr0, ys0, yr0, xs1, xr1, ys1, yr1, zs, zr, tot, fin,
    in_sem, w_recv, w_send, c_recv, r_recv, h_recv, r_send, z_recv, f_recv,
):
    slots, features = og.shape
    own_rows = wt.shape[0]
    units = wt.shape[1]
    region = 2 * own_rows
    chunk = 3 * LANES
    chunks = features // chunk
    size = own_rows // SLICES
    slices = [pl.ds(i * size, size) for i in range(SLICES)]

    loads = [
        pltpu.make_async_copy(src, dst, in_sem.at[i])
        for i, (src, dst) in enumerate(
            ((weight, wt), (gate_up, gu), (route_weight, rw), (out_grad, og))
        )
    ]
    for copy in loads:
        copy.start()

    me_s, me_d = lax.axis_index("shard"), lax.axis_index("dp")
    z, y, x, c = me_s // 2, me_s % 2, me_d // 2, me_d % 2
    home = lax.rem(z, 2) == x
    away = jnp.logical_not(home)

    def device(zz, yy, xx, cc):
        return (zz * 2 + yy, xx * 2 + cc)

    to_x, to_y, to_c = device(z, y, 1 - x, c), device(z, 1 - y, x, c), device(z, y, x, 1 - c)
    others_z = [lax.rem(z + d, 4) for d in (1, 2, 3)]

    barrier = pltpu.get_barrier_semaphore()
    partners = [to_x, to_y, to_c] + [device(zz, y, x, c) for zz in others_z]
    for dev in partners:
        pl.semaphore_signal(barrier, inc=1, device_id=dev, device_id_type=pl.DeviceIdType.MESH)

    def rows(zz, yy):
        return pl.ds(pl.multiple_of((zz * 2 + yy) * own_rows, 16), own_rows)

    def rows_of(zz, yy, part):
        return pl.ds(pl.multiple_of((zz * 2 + yy) * own_rows + part.start, 16), part.size)

    pending = []
    count = {"w": 0, "r": 0}

    def begin(kind, src, dst, recv, dev, cond=None):
        sems = w_send if kind == "w" else r_send
        copy = pltpu.make_async_remote_copy(
            src_ref=src, dst_ref=dst, send_sem=sems.at[count[kind]], recv_sem=recv,
            device_id=dev, device_id_type=pl.DeviceIdType.MESH,
        )
        count[kind] += 1
        pending.append((copy, cond))
        if cond is None:
            copy.start()
        else:
            pl.when(cond)(copy.start)

    def arrived(ref, recv, cond=None):
        copy = pltpu.make_async_remote_copy(
            src_ref=ref, dst_ref=ref, send_sem=w_send.at[0], recv_sem=recv,
            device_id=to_x, device_id_type=pl.DeviceIdType.MESH,
        )
        if cond is None:
            copy.wait_recv()
        else:
            pl.when(cond)(copy.wait_recv)

    def w_piece(zz, yy, t, q):
        return wg.at[t, rows_of(zz, yy, slices[q])], w_recv.at[t, zz * 2 + yy, q]

    def w_give(zz, yy, t, q, dev, cond=None):
        ref, sem = w_piece(zz, yy, t, q)
        begin("w", ref, ref, sem, dev, cond)

    def w_take(zz, yy, t, q, cond=None):
        ref, sem = w_piece(zz, yy, t, q)
        arrived(ref, sem, cond)

    loads[0].wait()
    wg[0, rows(z, y), :] = wt[:, :LANES]
    wg[1, rows(z, y), :] = jnp.concatenate(
        [wt[:, LANES:], jnp.zeros((own_rows, 2 * LANES - units), BF16)], axis=1
    )
    loads[1].wait()
    loads[2].wait()

    def gates():
        gate, up = gu[:units, :].astype(F32), gu[units:, :].astype(F32)
        sig = jax.nn.sigmoid(gate)
        return gate, up, sig, gate * sig

    _, up, _, activated = gates()
    live_row = (lax.broadcasted_iota(jnp.int32, (1, slots), 1) < live_rows[0]).astype(F32)
    hidden = live_row * activated * up
    hid[...] = jnp.concatenate(
        [hidden, jnp.zeros((2 * LANES - units, slots), F32)], axis=0
    ).T.astype(BF16)
    live = (lax.broadcasted_iota(jnp.int32, (slots, LANES), 0) < live_rows[0]).astype(F32)
    scale = jnp.broadcast_to(rw[...], (LANES, slots)).T
    wide = jnp.concatenate([live * scale] * 3, axis=1)
    loads[3].wait()

    def partial(i, carry):
        at = pl.ds(pl.multiple_of(i * chunk, LANES), chunk)
        g = (wide * og[:, at].astype(F32)).astype(BF16)
        gf[:, at] = g
        p = lax.dot_general(g, hid[...], (((0,), (0,)), ((), ())), preferred_element_type=F32)
        for t in (0, 1):
            part = p[:, t * LANES:(t + 1) * LANES]
            acc[t, at, :] = part
            psend[t, at, :] = part.astype(BF16)
        return carry

    lax.fori_loop(0, chunks, partial, 0)
    pl.semaphore_wait(barrier, len(partners))

    zk = [x, x + 2]
    far = [zk[0] != z, zk[1] != z]
    near = [zk[0] == z, zk[1] == z]
    across = [lax.rem(z + 2, 4), 3 - z, z + 1 - 2 * lax.rem(z, 2)]

    for k in (0, 1):
        part = pl.ds(2 * k * region, 2 * region)
        begin("r", psend.at[1 - c, part], crecv.at[part], c_recv.at[k], to_c)

    for q in range(SLICES):
        for zz in across:
            w_give(z, y, c, q, device(zz, y, x, c), home)

    def pair(u, k, yy, part):
        at = rows_of(u + 2 * k, yy, part)
        return acc[c, at, :] + crecv[at, :].astype(F32)

    def sum_first(q):
        part = slices[q]
        for i in (0, 1):
            yy, t = ((1 - y, 1 - x), (y, x))[i]
            xs0[i, part, :] = pair(1 - x, 0, yy, part).astype(BF16)
            begin("r", xs0.at[i, part], xr0.at[i, part], r_recv.at[0, i, q], to_x)
            ys1[i, part, :] = pair(t, 1, 1 - y, part).astype(BF16)
            begin("r", ys1.at[i, part], yr1.at[i, part], r_recv.at[1, i, q], to_y)

    def sum_second(q):
        part = slices[q]
        arrived(xr0.at[0, part], r_recv.at[0, 0, q])
        ys0[part, :] = (pair(x, 0, 1 - y, part) + xr0[0, part, :].astype(F32)).astype(BF16)
        begin("r", ys0.at[part], yr0.at[part], h_recv.at[0, q], to_y)
        arrived(yr1.at[0, part], r_recv.at[1, 0, q])
        xs1[part, :] = (pair(1 - x, 1, y, part) + yr1[0, part, :].astype(F32)).astype(BF16)
        begin("r", xs1.at[part], xr1.at[part], h_recv.at[1, q], to_x)

    def sum_z(q):
        part = slices[q]
        for k, (first, second) in enumerate(((xr0, yr0), (yr1, xr1))):
            arrived(first.at[1, part], r_recv.at[k, 1, q])
            arrived(second.at[part], h_recv.at[k, q])
            total = (
                pair(x, k, y, part) + first[1, part, :].astype(F32) + second[part, :].astype(F32)
            )
            zs[k, part, :] = total.astype(BF16)
            begin("r", zs.at[k, part], zr.at[z, part], z_recv.at[q, z], device(zk[k], y, x, c), far[k])

            @pl.when(near[k])
            def _():
                tot[part, :] = total

    def sum_owner(q):
        part = slices[q]

        @pl.when(home)
        def _():
            total = tot[part, :]
            for zz in others_z:
                arrived(zr.at[zz, part], z_recv.at[q, zz])
                total = total + zr[zz, part, :].astype(F32)
            fin[c, part, :] = total.astype(BF16)

        begin("r", fin.at[c, part], fin.at[c, part], f_recv.at[q, c], to_x, home)
        begin("r", fin.at[c, part], fin.at[c, part], f_recv.at[q, c], to_c, home)

    def other(q, u, k, yy):
        zz = u + 2 * k
        own = jnp.logical_and(zz == z, yy == y)
        w_give(zz, yy, c, q, to_c, jnp.logical_not(own))

    def gather_first(q):
        for k, order in ((0, (to_y, to_x)), (1, (to_x, to_y))):
            w_take(zk[k], y, c, q, far[k])
            for dev in order:
                w_give(zk[k], y, c, q, dev, far[k] if dev is to_x else None)
            other(q, x, k, y)

    def gather_second(q):
        w_take(zk[0], 1 - y, c, q)
        w_give(zk[0], 1 - y, c, q, to_x)
        w_take(zk[1] + 1 - 2 * x, y, c, q, zk[1] + 1 - 2 * x != z)
        w_give(zk[1] + 1 - 2 * x, y, c, q, to_y)
        other(q, x, 0, 1 - y)
        other(q, 1 - x, 1, y)
        w_take(zk[0] + 1 - 2 * x, y, c, q, zk[0] + 1 - 2 * x != z)
        other(q, 1 - x, 0, y)
        w_take(zk[1], 1 - y, c, q)
        other(q, x, 1, 1 - y)

    def gather_last(q):
        for k in (0, 1):
            w_take(zk[k] + 1 - 2 * x, 1 - y, c, q)
            other(q, 1 - x, k, 1 - y)

    def gather_end(q):
        for zz in range(4):
            for yy in (0, 1):
                own = jnp.logical_and(zz == z, yy == y)
                w_take(zz, yy, 1 - c, q, jnp.logical_not(own))

    for k in (0, 1):
        arrived(crecv.at[pl.ds(2 * k * region, 2 * region)], c_recv.at[k])

    sum_first(0)
    sum_first(1)
    gather_first(0)
    sum_second(0)
    sum_first(2)
    gather_first(1)
    gather_second(0)
    sum_second(1)
    sum_z(0)
    gather_first(2)
    sum_second(2)
    gather_second(1)
    sum_z(1)
    gather_last(0)
    gather_second(2)
    sum_z(2)
    gather_last(1)
    sum_owner(0)
    gather_last(2)
    sum_owner(1)
    sum_owner(2)
    gather_end(0)
    gather_end(1)
    gather_end(2)

    wide_route = jnp.concatenate([scale] * 3, axis=1)

    def outputs(i, carry):
        grad_hidden, route = carry
        at = pl.ds(pl.multiple_of(i * chunk, LANES), chunk)
        w = jnp.concatenate([wg[0, at, :], wg[1, at, :]], axis=1)
        full = lax.dot_general(hid[...], w, (((1,), (1,)), ((), ())), preferred_element_type=F32)
        eo[:, at] = (wide_route * full).astype(BF16)
        prod = og[:, at].astype(F32) * full
        route = route + prod[:, :LANES] + prod[:, LANES:2 * LANES] + prod[:, 2 * LANES:]
        grad_hidden = grad_hidden + jnp.dot(gf[:, at], w, preferred_element_type=F32)
        return grad_hidden, route

    carry = (jnp.zeros((slots, 2 * LANES), F32), jnp.zeros((slots, LANES), F32))
    carry = lax.fori_loop(0, chunks // 2, outputs, carry)
    for q, part in enumerate(slices):
        arrived(fin.at[c, part], f_recv.at[q, c], away)
        begin("r", fin.at[c, part], fin.at[c, part], f_recv.at[q, c], to_c, away)
    grad_hidden, route = lax.fori_loop(chunks // 2, chunks, outputs, carry)
    grad_route[...] = jnp.sum((live * route).T, axis=0, keepdims=True)
    gate, up, sig, activated = gates()
    grad_hidden = grad_hidden.T[:units, :]
    grad_gate_up[:units, :] = (grad_hidden * up * sig * (1.0 + gate * (1.0 - sig))).astype(BF16)
    grad_gate_up[units:, :] = (grad_hidden * activated).astype(BF16)

    for q, part in enumerate(slices):
        arrived(fin.at[1 - c, part], f_recv.at[q, 1 - c])
    grad_down[:, :LANES] = fin[0].astype(F32)
    grad_down[:, LANES:] = fin[1].astype(F32)[:, :units - LANES]

    for copy, cond in pending:
        if cond is None:
            copy.wait_send()
        else:
            pl.when(cond)(copy.wait_send)


def place(*refs):
    count = (len(refs) - 1) // 2
    copies = [
        pltpu.make_async_copy(refs[i], refs[count + i], refs[-1].at[i]) for i in range(count)
    ]
    for copy in copies:
        copy.start()
    for copy in copies:
        copy.wait()


def fused(gate_up, route_weight, live_rows, down_weight, out_grad):
    slots, features = out_grad.shape
    own_rows, units = down_weight.shape
    region = 2 * own_rows
    vmem = pl.BlockSpec(memory_space=pltpu.VMEM)
    hbm = pl.BlockSpec(memory_space=pltpu.HBM)
    dma = pltpu.SemaphoreType.DMA
    piece = (own_rows, LANES)
    shapes = (
        jax.ShapeDtypeStruct((slots, features), BF16),
        jax.ShapeDtypeStruct((2 * units, slots), BF16),
        jax.ShapeDtypeStruct((1, slots), F32),
        jax.ShapeDtypeStruct((own_rows, units), F32),
    )
    results = pl.pallas_call(
        kernel,
        out_shape=tuple(pltpu.VMEM(a.shape, a.dtype) for a in shapes),
        in_specs=[hbm, hbm, pl.BlockSpec(memory_space=pltpu.SMEM), hbm, hbm],
        out_specs=(vmem,) * 4,
        scratch_shapes=[
            pltpu.VMEM((slots, features), BF16),
            pltpu.VMEM((2 * units, slots), BF16),
            pltpu.VMEM((1, slots), F32),
            pltpu.VMEM((own_rows, units), BF16),
            pltpu.VMEM((slots, features), BF16),
            pltpu.VMEM((slots, 2 * LANES), BF16),
            pltpu.VMEM((2, features, LANES), BF16),
            pltpu.VMEM((2, features, LANES), F32),
            pltpu.VMEM((2, features, LANES), BF16),
            pltpu.VMEM((features, LANES), BF16),
            pltpu.VMEM((2,) + piece, BF16),
            pltpu.VMEM((2,) + piece, BF16),
            pltpu.VMEM(piece, BF16),
            pltpu.VMEM(piece, BF16),
            pltpu.VMEM(piece, BF16),
            pltpu.VMEM(piece, BF16),
            pltpu.VMEM((2,) + piece, BF16),
            pltpu.VMEM((2,) + piece, BF16),
            pltpu.VMEM((2,) + piece, BF16),
            pltpu.VMEM((4,) + piece, BF16),
            pltpu.VMEM(piece, F32),
            pltpu.VMEM((2,) + piece, BF16),
            dma((4,)), dma((2, 8, SLICES)), dma((22 * SLICES,)), dma((2,)), dma((2, 2, SLICES)),
            dma((2, SLICES)), dma((4 + 11 * SLICES,)), dma((SLICES, 4)), dma((SLICES, 2)),
        ],
        compiler_params=pltpu.CompilerParams(
            collective_id=0, has_side_effects=True, vmem_limit_bytes=58 * 2**20
        ),
        cost_estimate=pl.CostEstimate(
            flops=6 * slots * features * units, bytes_accessed=6 * slots * features, transcendentals=0
        ),
    )(gate_up.T, route_weight.reshape(1, slots), live_rows, down_weight, out_grad)
    expert_out, grad_gate_up, grad_route, grad_down = pl.pallas_call(
        place,
        out_shape=shapes,
        in_specs=[pl.BlockSpec(memory_space=pl.ANY)] * 4,
        out_specs=(hbm,) * 4,
        scratch_shapes=[dma((4,))],
        compiler_params=pltpu.CompilerParams(vmem_limit_bytes=2**20),
    )(*results)
    return expert_out, grad_gate_up.T, grad_route.reshape(slots), grad_down


def plain(gate_up, route_weight, live_rows, down_weight, out_grad):
    slot_count = gate_up.shape[0]
    hidden_units = gate_up.shape[1] // 2
    row_mask = (lax.iota(jnp.int32, slot_count) < live_rows[0]).astype(jnp.float32)[:, None]
    gate_pre = gate_up[:, :hidden_units].astype(jnp.float32)
    up_proj = gate_up[:, hidden_units:].astype(jnp.float32)
    sigmoid_gate = jax.nn.sigmoid(gate_pre)
    activated = gate_pre * sigmoid_gate
    hidden = (row_mask * activated * up_proj).astype(jnp.bfloat16)
    row_scale = route_weight[:, None]
    gathered = lax.all_gather(down_weight, "shard", axis=0, tiled=True)
    full = lax.dot_general(
        hidden, gathered, (((1,), (1,)), ((), ())), preferred_element_type=jnp.float32
    )
    expert_out = (row_scale * full).astype(jnp.bfloat16)
    grad_route = row_mask[:, 0] * jnp.sum(out_grad.astype(jnp.float32) * full, axis=1)
    grad_full = (row_mask * row_scale * out_grad.astype(jnp.float32)).astype(jnp.bfloat16)
    grad_hidden = jnp.dot(grad_full, gathered, preferred_element_type=jnp.float32)
    grad_gate = grad_hidden * up_proj * sigmoid_gate * (1.0 + gate_pre * (1.0 - sigmoid_gate))
    grad_up = grad_hidden * activated
    grad_gate_up = jnp.concatenate([grad_gate, grad_up], axis=1).astype(jnp.bfloat16)
    owned = lax.psum_scatter(
        lax.dot_general(
            grad_full, hidden, (((0,), (0,)), ((), ())), preferred_element_type=jnp.float32
        ),
        "shard",
        scatter_dimension=0,
        tiled=True,
    )
    grad_down = lax.psum(owned, "dp")
    return (expert_out, grad_gate_up, grad_route, grad_down)


def solution(mesh):
    shape = (mesh.shape["shard"], mesh.shape["dp"])
    in_specs = (
        P(("shard", "dp"), None),
        P(("shard", "dp")),
        P(("shard", "dp")),
        P("shard", None),
        P(("shard", "dp"), None),
    )
    out_specs = (
        P(("shard", "dp"), None),
        P(("shard", "dp"), None),
        P(("shard", "dp")),
        P("shard", None),
    )
    return jax.shard_map(
        fused if shape == (8, 4) else plain,
        mesh=mesh, in_specs=in_specs, out_specs=out_specs, check_vma=False,
    )
```

```python
import jax
import jax.numpy as jnp
from jax import lax
from jax.experimental import pallas as pl
from jax.experimental.pallas import tpu as pltpu
from jax.sharding import PartitionSpec as P

LANES = 128
SLICES = 3
F32 = jnp.float32
BF16 = jnp.bfloat16


def kernel(
    gate_up, route_weight, live_rows, weight, out_grad,
    eo, grad_gate_up, grad_route, grad_down,
    og, gu, rw, wt, gf, hid, wg, acc, psend, crecv,
    xs0, xr0, ys0, yr0, xs1, xr1, ys1, yr1, zs, zr, tot, fin,
    in_sem, w_recv, w_send, c_recv, r_recv, h_recv, r_send, z_recv, f_recv,
):
    slots, features = og.shape
    own_rows = wt.shape[0]
    units = wt.shape[1]
    region = 2 * own_rows
    chunk = 3 * LANES
    chunks = features // chunk
    size = own_rows // SLICES
    slices = [pl.ds(i * size, size) for i in range(SLICES)]

    loads = [
        pltpu.make_async_copy(src, dst, in_sem.at[i])
        for i, (src, dst) in enumerate(
            ((weight, wt), (gate_up, gu), (route_weight, rw), (out_grad, og))
        )
    ]
    for copy in loads:
        copy.start()

    me_s, me_d = lax.axis_index("shard"), lax.axis_index("dp")
    z, y, x, c = me_s // 2, me_s % 2, me_d // 2, me_d % 2
    home = lax.rem(z, 2) == x
    away = jnp.logical_not(home)

    def device(zz, yy, xx, cc):
        return (zz * 2 + yy, xx * 2 + cc)

    to_x, to_y, to_c = device(z, y, 1 - x, c), device(z, 1 - y, x, c), device(z, y, x, 1 - c)
    others_z = [lax.rem(z + d, 4) for d in (1, 2, 3)]

    barrier = pltpu.get_barrier_semaphore()
    partners = [to_x, to_y, to_c] + [device(zz, y, x, c) for zz in others_z]
    for dev in partners:
        pl.semaphore_signal(barrier, inc=1, device_id=dev, device_id_type=pl.DeviceIdType.MESH)

    def rows(zz, yy):
        return pl.ds(pl.multiple_of((zz * 2 + yy) * own_rows, 16), own_rows)

    def rows_of(zz, yy, part):
        return pl.ds(pl.multiple_of((zz * 2 + yy) * own_rows + part.start, 16), part.size)

    pending = []
    count = {"w": 0, "r": 0}

    def begin(kind, src, dst, recv, dev, cond=None):
        sems = w_send if kind == "w" else r_send
        copy = pltpu.make_async_remote_copy(
            src_ref=src, dst_ref=dst, send_sem=sems.at[count[kind]], recv_sem=recv,
            device_id=dev, device_id_type=pl.DeviceIdType.MESH,
        )
        count[kind] += 1
        pending.append((copy, cond))
        if cond is None:
            copy.start()
        else:
            pl.when(cond)(copy.start)

    def arrived(ref, recv, cond=None):
        copy = pltpu.make_async_remote_copy(
            src_ref=ref, dst_ref=ref, send_sem=w_send.at[0], recv_sem=recv,
            device_id=to_x, device_id_type=pl.DeviceIdType.MESH,
        )
        if cond is None:
            copy.wait_recv()
        else:
            pl.when(cond)(copy.wait_recv)

    def w_piece(zz, yy, t, q):
        return wg.at[t, rows_of(zz, yy, slices[q])], w_recv.at[t, zz * 2 + yy, q]

    def w_give(zz, yy, t, q, dev, cond=None):
        ref, sem = w_piece(zz, yy, t, q)
        begin("w", ref, ref, sem, dev, cond)

    def w_take(zz, yy, t, q, cond=None):
        ref, sem = w_piece(zz, yy, t, q)
        arrived(ref, sem, cond)

    loads[0].wait()
    wg[0, rows(z, y), :] = wt[:, :LANES]
    wg[1, rows(z, y), :] = jnp.concatenate(
        [wt[:, LANES:], jnp.zeros((own_rows, 2 * LANES - units), BF16)], axis=1
    )
    loads[1].wait()
    loads[2].wait()

    def gates():
        gate, up = gu[:units, :].astype(F32), gu[units:, :].astype(F32)
        sig = jax.nn.sigmoid(gate)
        return gate, up, sig, gate * sig

    _, up, _, activated = gates()
    live_row = (lax.broadcasted_iota(jnp.int32, (1, slots), 1) < live_rows[0]).astype(F32)
    hidden = live_row * activated * up
    hid[...] = jnp.concatenate(
        [hidden, jnp.zeros((2 * LANES - units, slots), F32)], axis=0
    ).T.astype(BF16)
    live = (lax.broadcasted_iota(jnp.int32, (slots, LANES), 0) < live_rows[0]).astype(F32)
    scale = jnp.broadcast_to(rw[...], (LANES, slots)).T
    wide = jnp.concatenate([live * scale] * 3, axis=1)
    loads[3].wait()

    def partial(i, carry):
        at = pl.ds(pl.multiple_of(i * chunk, LANES), chunk)
        g = (wide * og[:, at].astype(F32)).astype(BF16)
        gf[:, at] = g
        p = lax.dot_general(g, hid[...], (((0,), (0,)), ((), ())), preferred_element_type=F32)
        for t in (0, 1):
            part = p[:, t * LANES:(t + 1) * LANES]
            acc[t, at, :] = part
            psend[t, at, :] = part.astype(BF16)
        return carry

    lax.fori_loop(0, chunks, partial, 0)
    pl.semaphore_wait(barrier, len(partners))

    zk = [x, x + 2]
    far = [zk[0] != z, zk[1] != z]
    near = [zk[0] == z, zk[1] == z]
    across = [lax.rem(z + 2, 4), 3 - z, z + 1 - 2 * lax.rem(z, 2)]

    for k in (0, 1):
        part = pl.ds(2 * k * region, 2 * region)
        begin("r", psend.at[1 - c, part], crecv.at[part], c_recv.at[k], to_c)

    for q in range(SLICES):
        for zz in across:
            w_give(z, y, c, q, device(zz, y, x, c), home)
        w_give(z, y, c, q, to_y, jnp.logical_or(home, z >= 2))

    def pair(u, k, yy, part):
        at = rows_of(u + 2 * k, yy, part)
        return acc[c, at, :] + crecv[at, :].astype(F32)

    def sum_first(q):
        part = slices[q]
        for i in (0, 1):
            yy, t = ((1 - y, 1 - x), (y, x))[i]
            xs0[i, part, :] = pair(1 - x, 0, yy, part).astype(BF16)
            begin("r", xs0.at[i, part], xr0.at[i, part], r_recv.at[0, i, q], to_x)
            ys1[i, part, :] = pair(t, 1, 1 - y, part).astype(BF16)
            begin("r", ys1.at[i, part], yr1.at[i, part], r_recv.at[1, i, q], to_y)

    def sum_second(q):
        part = slices[q]
        arrived(xr0.at[0, part], r_recv.at[0, 0, q])
        ys0[part, :] = (pair(x, 0, 1 - y, part) + xr0[0, part, :].astype(F32)).astype(BF16)
        begin("r", ys0.at[part], yr0.at[part], h_recv.at[0, q], to_y)
        arrived(yr1.at[0, part], r_recv.at[1, 0, q])
        xs1[part, :] = (pair(1 - x, 1, y, part) + yr1[0, part, :].astype(F32)).astype(BF16)
        begin("r", xs1.at[part], xr1.at[part], h_recv.at[1, q], to_x)

    def sum_z(q):
        part = slices[q]
        for k, (first, second) in enumerate(((xr0, yr0), (yr1, xr1))):
            arrived(first.at[1, part], r_recv.at[k, 1, q])
            arrived(second.at[part], h_recv.at[k, q])
            total = (
                pair(x, k, y, part) + first[1, part, :].astype(F32) + second[part, :].astype(F32)
            )
            zs[k, part, :] = total.astype(BF16)
            begin("r", zs.at[k, part], zr.at[z, part], z_recv.at[q, z], device(zk[k], y, x, c), far[k])

            @pl.when(near[k])
            def _():
                tot[part, :] = total

    def sum_owner(q):
        part = slices[q]

        @pl.when(home)
        def _():
            total = tot[part, :]
            for zz in others_z:
                arrived(zr.at[zz, part], z_recv.at[q, zz])
                total = total + zr[zz, part, :].astype(F32)
            fin[c, part, :] = total.astype(BF16)

        begin("r", fin.at[c, part], fin.at[c, part], f_recv.at[q, c], to_x, home)
        begin("r", fin.at[c, part], fin.at[c, part], f_recv.at[q, c], to_c, home)

    def other(q, u, k, yy):
        zz = u + 2 * k
        own = jnp.logical_and(zz == z, yy == y)
        w_give(zz, yy, c, q, to_c, jnp.logical_not(own))

    def gather_first(q):
        for k, order in ((0, (to_y, to_x)), (1, (to_x, to_y))):
            w_take(zk[k], y, c, q, far[k])
            for dev in order:
                w_give(zk[k], y, c, q, dev, far[k])
            other(q, x, k, y)

    def gather_second(q):
        w_take(zk[0], 1 - y, c, q)
        w_give(zk[0], 1 - y, c, q, to_x)
        w_take(zk[1] + 1 - 2 * x, y, c, q, zk[1] + 1 - 2 * x != z)
        w_give(zk[1] + 1 - 2 * x, y, c, q, to_y, zk[1] + 1 - 2 * x != z)
        other(q, x, 0, 1 - y)
        other(q, 1 - x, 1, y)
        w_take(zk[0] + 1 - 2 * x, y, c, q, zk[0] + 1 - 2 * x != z)
        other(q, 1 - x, 0, y)
        w_take(zk[1], 1 - y, c, q)
        other(q, x, 1, 1 - y)

    def gather_last(q):
        for k in (0, 1):
            w_take(zk[k] + 1 - 2 * x, 1 - y, c, q)
            other(q, 1 - x, k, 1 - y)

    def gather_end(q):
        for zz in range(4):
            for yy in (0, 1):
                own = jnp.logical_and(zz == z, yy == y)
                w_take(zz, yy, 1 - c, q, jnp.logical_not(own))

    for k in (0, 1):
        arrived(crecv.at[pl.ds(2 * k * region, 2 * region)], c_recv.at[k])

    sum_first(0)
    sum_first(1)
    sum_second(0)
    gather_first(0)
    sum_first(2)
    sum_second(1)
    gather_first(1)
    sum_z(0)
    gather_second(0)
    sum_second(2)
    gather_first(2)
    sum_z(1)
    gather_last(0)
    gather_second(1)
    sum_z(2)
    gather_last(1)
    gather_second(2)
    gather_last(2)
    sum_owner(0)
    sum_owner(1)
    sum_owner(2)
    gather_end(0)
    gather_end(1)
    gather_end(2)

    wide_route = jnp.concatenate([scale] * 3, axis=1)

    def outputs(i, carry):
        grad_hidden, route = carry
        at = pl.ds(pl.multiple_of(i * chunk, LANES), chunk)
        w = jnp.concatenate([wg[0, at, :], wg[1, at, :]], axis=1)
        full = lax.dot_general(hid[...], w, (((1,), (1,)), ((), ())), preferred_element_type=F32)
        eo[:, at] = (wide_route * full).astype(BF16)
        prod = og[:, at].astype(F32) * full
        route = route + prod[:, :LANES] + prod[:, LANES:2 * LANES] + prod[:, 2 * LANES:]
        grad_hidden = grad_hidden + jnp.dot(gf[:, at], w, preferred_element_type=F32)
        return grad_hidden, route

    carry = (jnp.zeros((slots, 2 * LANES), F32), jnp.zeros((slots, LANES), F32))
    carry = lax.fori_loop(0, chunks // 2, outputs, carry)
    for q, part in enumerate(slices):
        arrived(fin.at[c, part], f_recv.at[q, c], away)
        begin("r", fin.at[c, part], fin.at[c, part], f_recv.at[q, c], to_c, away)
    grad_hidden, route = lax.fori_loop(chunks // 2, chunks, outputs, carry)
    grad_route[...] = jnp.sum((live * route).T, axis=0, keepdims=True)
    gate, up, sig, activated = gates()
    grad_hidden = grad_hidden.T[:units, :]
    grad_gate_up[:units, :] = (grad_hidden * up * sig * (1.0 + gate * (1.0 - sig))).astype(BF16)
    grad_gate_up[units:, :] = (grad_hidden * activated).astype(BF16)

    for q, part in enumerate(slices):
        arrived(fin.at[1 - c, part], f_recv.at[q, 1 - c])
    grad_down[:, :LANES] = fin[0].astype(F32)
    grad_down[:, LANES:] = fin[1].astype(F32)[:, :units - LANES]

    for copy, cond in pending:
        if cond is None:
            copy.wait_send()
        else:
            pl.when(cond)(copy.wait_send)


def place(*refs):
    count = (len(refs) - 1) // 2
    copies = [
        pltpu.make_async_copy(refs[i], refs[count + i], refs[-1].at[i]) for i in range(count)
    ]
    for copy in copies:
        copy.start()
    for copy in copies:
        copy.wait()


def fused(gate_up, route_weight, live_rows, down_weight, out_grad):
    slots, features = out_grad.shape
    own_rows, units = down_weight.shape
    region = 2 * own_rows
    vmem = pl.BlockSpec(memory_space=pltpu.VMEM)
    hbm = pl.BlockSpec(memory_space=pltpu.HBM)
    dma = pltpu.SemaphoreType.DMA
    piece = (own_rows, LANES)
    shapes = (
        jax.ShapeDtypeStruct((slots, features), BF16),
        jax.ShapeDtypeStruct((2 * units, slots), BF16),
        jax.ShapeDtypeStruct((1, slots), F32),
        jax.ShapeDtypeStruct((own_rows, units), F32),
    )
    results = pl.pallas_call(
        kernel,
        out_shape=tuple(pltpu.VMEM(a.shape, a.dtype) for a in shapes),
        in_specs=[hbm, hbm, pl.BlockSpec(memory_space=pltpu.SMEM), hbm, hbm],
        out_specs=(vmem,) * 4,
        scratch_shapes=[
            pltpu.VMEM((slots, features), BF16),
            pltpu.VMEM((2 * units, slots), BF16),
            pltpu.VMEM((1, slots), F32),
            pltpu.VMEM((own_rows, units), BF16),
            pltpu.VMEM((slots, features), BF16),
            pltpu.VMEM((slots, 2 * LANES), BF16),
            pltpu.VMEM((2, features, LANES), BF16),
            pltpu.VMEM((2, features, LANES), F32),
            pltpu.VMEM((2, features, LANES), BF16),
            pltpu.VMEM((features, LANES), BF16),
            pltpu.VMEM((2,) + piece, BF16),
            pltpu.VMEM((2,) + piece, BF16),
            pltpu.VMEM(piece, BF16),
            pltpu.VMEM(piece, BF16),
            pltpu.VMEM(piece, BF16),
            pltpu.VMEM(piece, BF16),
            pltpu.VMEM((2,) + piece, BF16),
            pltpu.VMEM((2,) + piece, BF16),
            pltpu.VMEM((2,) + piece, BF16),
            pltpu.VMEM((4,) + piece, BF16),
            pltpu.VMEM(piece, F32),
            pltpu.VMEM((2,) + piece, BF16),
            dma((4,)), dma((2, 8, SLICES)), dma((22 * SLICES,)), dma((2,)), dma((2, 2, SLICES)),
            dma((2, SLICES)), dma((4 + 11 * SLICES,)), dma((SLICES, 4)), dma((SLICES, 2)),
        ],
        compiler_params=pltpu.CompilerParams(
            collective_id=0, has_side_effects=True, vmem_limit_bytes=58 * 2**20
        ),
        cost_estimate=pl.CostEstimate(
            flops=6 * slots * features * units, bytes_accessed=6 * slots * features, transcendentals=0
        ),
    )(gate_up.T, route_weight.reshape(1, slots), live_rows, down_weight, out_grad)
    expert_out, grad_gate_up, grad_route, grad_down = pl.pallas_call(
        place,
        out_shape=shapes,
        in_specs=[pl.BlockSpec(memory_space=pl.ANY)] * 4,
        out_specs=(hbm,) * 4,
        scratch_shapes=[dma((4,))],
        compiler_params=pltpu.CompilerParams(vmem_limit_bytes=2**20),
    )(*results)
    return expert_out, grad_gate_up.T, grad_route.reshape(slots), grad_down


def plain(gate_up, route_weight, live_rows, down_weight, out_grad):
    slot_count = gate_up.shape[0]
    hidden_units = gate_up.shape[1] // 2
    row_mask = (lax.iota(jnp.int32, slot_count) < live_rows[0]).astype(jnp.float32)[:, None]
    gate_pre = gate_up[:, :hidden_units].astype(jnp.float32)
    up_proj = gate_up[:, hidden_units:].astype(jnp.float32)
    sigmoid_gate = jax.nn.sigmoid(gate_pre)
    activated = gate_pre * sigmoid_gate
    hidden = (row_mask * activated * up_proj).astype(jnp.bfloat16)
    row_scale = route_weight[:, None]
    gathered = lax.all_gather(down_weight, "shard", axis=0, tiled=True)
    full = lax.dot_general(
        hidden, gathered, (((1,), (1,)), ((), ())), preferred_element_type=jnp.float32
    )
    expert_out = (row_scale * full).astype(jnp.bfloat16)
    grad_route = row_mask[:, 0] * jnp.sum(out_grad.astype(jnp.float32) * full, axis=1)
    grad_full = (row_mask * row_scale * out_grad.astype(jnp.float32)).astype(jnp.bfloat16)
    grad_hidden = jnp.dot(grad_full, gathered, preferred_element_type=jnp.float32)
    grad_gate = grad_hidden * up_proj * sigmoid_gate * (1.0 + gate_pre * (1.0 - sigmoid_gate))
    grad_up = grad_hidden * activated
    grad_gate_up = jnp.concatenate([grad_gate, grad_up], axis=1).astype(jnp.bfloat16)
    owned = lax.psum_scatter(
        lax.dot_general(
            grad_full, hidden, (((0,), (0,)), ((), ())), preferred_element_type=jnp.float32
        ),
        "shard",
        scatter_dimension=0,
        tiled=True,
    )
    grad_down = lax.psum(owned, "dp")
    return (expert_out, grad_gate_up, grad_route, grad_down)


def solution(mesh):
    shape = (mesh.shape["shard"], mesh.shape["dp"])
    in_specs = (
        P(("shard", "dp"), None),
        P(("shard", "dp")),
        P(("shard", "dp")),
        P("shard", None),
        P(("shard", "dp"), None),
    )
    out_specs = (
        P(("shard", "dp"), None),
        P(("shard", "dp"), None),
        P(("shard", "dp")),
        P("shard", None),
    )
    return jax.shard_map(
        fused if shape == (8, 4) else plain,
        mesh=mesh, in_specs=in_specs, out_specs=out_specs, check_vma=False,
    )
```
